256 devices in a mesh: ao: 128 (over x, z, y), aux: 2 (over core).
Axes of the slice: x: 4, y: 4, z: 8, core: 2. Of those that a mesh axis runs over, the one named last changes fastest.
Arguments:
- factors: bfloat16 [2, 196608, 3000], P('aux', 'ao'), may hold values from -1.75 to 1.75
- pair_keep: int32 [768, 2], P('ao'), may hold values 0 or 1
Outputs:
- upper_band: float32 [196608, 768], P(('ao', 'aux'))
- lower_band: float32 [196608, 512], P(('ao', 'aux'))
The draws below stay inside these ranges and needn't reach their ends.
All inputs are finite; a program needn't handle non-finite values. No bound on the sum of `pair_keep` on one device may be relied on, other than what follows from the above.
Results may differ from the reference program's by a relative error of at most 0.0003.
Values may be sent and summed in bfloat16 or wider, within the bound.
No kernel may reach another device: no remote copies, remote signals or barrier semaphores. Data moves between devices by JAX's collectives and lax.ppermute only.
A program may use at most 128 MiB of HBM per device.

```python
import jax
import jax.numpy as jnp
from jax import lax

BS = 256
NOCC = 3000
REACH = 2
NBLK = 768
NAUX = 2
NAO = 196608


def set_ends(array, key, least, top_value):
    shape = array.shape
    place = [jax.random.randint(jax.random.fold_in(key, axis), (), 0, shape[axis]) for axis in range(len(shape))]
    array = array.at[tuple(place)].set(least)
    longest = shape.index(max(shape))
    place[longest] = (place[longest] + 1) % shape[longest]
    return array.at[tuple(place)].set(top_value)


def steps_of(rng, extent, pieces, smallest, top_value):
    loudness, own = 1.0, jax.random.fold_in(rng, 6)
    for position, parts in pieces:
        draws = jnp.exp(jax.random.uniform(jax.random.fold_in(own, position), (parts,), jnp.float32, smallest / len(pieces), top_value / len(pieces)))
        loudness = loudness * jnp.repeat(draws, extent[position] // parts).reshape([-1 if axis == position else 1 for axis in range(len(extent))])
    return loudness


def centred(key, dims, width, most, split=(), kind=jnp.bfloat16):
    result = width * jax.random.normal(key, dims, jnp.float32)
    if split:
        result = result * steps_of(key, dims, split, -0.22, 0.18)
    return jnp.clip(result, -most, most).astype(kind)


def setup_inputs(seed: int = 0) -> dict:
    splits = jax.random.split(jax.random.key(seed), 3)
    factors = centred(splits[0], (NAUX, NAO, NOCC), ((NAUX * NOCC) ** -0.25), 1.75, ((0, 2), (1, 128)))
    pair_keep = set_ends((jax.random.randint(splits[1], (NBLK, REACH), 0, 2) < 1).astype(jnp.int32), jax.random.fold_in(splits[1], 1), 0, 1)
    return dict(factors=factors, pair_keep=pair_keep)


def reference(factors, pair_keep):
    blocks = factors.reshape(NAUX, NBLK, BS, NOCC)
    padded = jnp.concatenate([blocks, jnp.zeros((NAUX, REACH, BS, NOCC), blocks.dtype)], axis=1)
    flags = jnp.concatenate([jnp.ones((NBLK, 1), jnp.int32), pair_keep.astype(jnp.int32)], axis=1)

    def per_block(index):
        own = lax.dynamic_index_in_dim(padded, index, 1, keepdims=False).astype(jnp.float32)
        tiles = []
        for offset in range(REACH + 1):
            other = lax.dynamic_index_in_dim(padded, index + offset, 1, keepdims=False).astype(jnp.float32)
            product = jnp.einsum("pai,pbi->ab", own, other)
            inside = (index + offset) < NBLK
            tiles.append(jnp.where((flags[index, offset] > 0) & inside, product, jnp.float32(0.0)))
        return jnp.concatenate(tiles, axis=1)

    upper = lax.map(per_block, jnp.arange(NBLK, dtype=jnp.int32))
    lower_parts = []
    for offset in range(1, REACH + 1):
        source = upper[:, :, offset * BS:(offset + 1) * BS]
        moved = jnp.concatenate([jnp.zeros((offset, BS, BS), jnp.float32), source], axis=0)[:NBLK]
        lower_parts.append(jnp.swapaxes(moved, 1, 2))
    lower = jnp.concatenate(lower_parts, axis=2)
    return upper.reshape(NAO, (REACH + 1) * BS), lower.reshape(NAO, REACH * BS)
```

```python
import functools

import jax
import jax.numpy as jnp
import numpy as np
from jax import lax
from jax.experimental import pallas as pl
from jax.experimental.pallas import tpu as pltpu
from jax.sharding import PartitionSpec as P

BS = 256
BLOCKS = 6
HALF = 128

KEPT = (
    ((0, 0), (0, 1), (0, 2), (1, 1), (1, 2), (2, 2), (1, 3), (2, 3), (2, 4)),
    ((1, 3), (2, 3), (2, 4), (3, 3), (3, 4), (3, 5), (4, 4), (4, 5), (5, 5)),
)
SLOTS = 9


def slot_table():
    table = np.full((2, 2, BLOCKS, 3), -1, np.int32)
    for core in range(2):
        for whose in range(2):
            for slot, (m, n) in enumerate(KEPT[core if whose == 0 else 1 - core]):
                table[core, whose, n, m - n + 2] = slot
    return table


def local_kernel(table, g_ref, keep_ref, give_ref, wide_ref, turned):
    n = pl.program_id(0)
    rows = pl.multiple_of((n + 2) * BS, BS)
    flipped = g_ref[...].T
    turned[pl.ds(rows, BS), :] = flipped

    @pl.when(n < 2)
    def _():
        wide_ref[pl.ds(pl.multiple_of((n + 2) * BS, BS), BS), :] = flipped

    @pl.when(n > 3)
    def _():
        wide_ref[pl.ds(pl.multiple_of((n - 4) * BS, BS), BS), :] = flipped

    left = turned[pl.ds(pl.multiple_of(n * BS, BS), 3 * BS), :]
    tiles = jnp.dot(left, g_ref[...], preferred_element_type=jnp.float32)
    for k in range(3):
        tile = tiles[k * BS:(k + 1) * BS]
        for whose, out in ((0, keep_ref), (1, give_ref)):
            slot = table[(whose * BLOCKS + n) * 3 + k]

            @pl.when(slot >= 0)
            def _():
                out[slot] = tile


def local_tiles(core, g):
    table = jnp.asarray(slot_table())[core].reshape(-1)
    nocc = g.shape[0]
    return pl.pallas_call(
        local_kernel,
        grid_spec=pltpu.PrefetchScalarGridSpec(
            num_scalar_prefetch=1,
            grid=(BLOCKS,),
            in_specs=[pl.BlockSpec((nocc, BS), lambda n, t: (0, n))],
            out_specs=[
                pl.BlockSpec((SLOTS, BS, BS), lambda n, t: (0, 0, 0)),
                pl.BlockSpec((SLOTS, BS, BS), lambda n, t: (0, 0, 0)),
                pl.BlockSpec((4 * BS, nocc), lambda n, t: (0, 0)),
            ],
            scratch_shapes=[pltpu.VMEM(((BLOCKS + 2) * BS, nocc), jnp.bfloat16)],
        ),
        out_shape=[
            jax.ShapeDtypeStruct((SLOTS, BS, BS), jnp.float32),
            jax.ShapeDtypeStruct((SLOTS, BS, BS), jnp.float32),
            jax.ShapeDtypeStruct((4 * BS, nocc), jnp.bfloat16),
        ],
        compiler_params=pltpu.CompilerParams(vmem_limit_bytes=48 * 1024 * 1024),
        cost_estimate=pl.CostEstimate(
            flops=7_000_000_000, bytes_accessed=20_000_000, transcendentals=0
        ),
        name="local_tiles",
    )(table, g)


def edge_kernel(core, wide_ref, down_ref, up_ref, own_ref, give_ref):
    low = jnp.dot(wide_ref[2 * BS:, :], up_ref[...], preferred_element_type=jnp.float32)
    high = jnp.dot(wide_ref[:2 * BS, :], down_ref[...], preferred_element_type=jnp.float32)
    first = core[0] == 0
    own_ref[...] = jnp.where(first, low, high)
    give_ref[...] = jnp.where(first, high, low)


def edge_tiles(core, wide, down, up):
    smem = pl.BlockSpec(memory_space=pltpu.SMEM)
    vmem = pl.BlockSpec(memory_space=pltpu.VMEM)
    out = jax.ShapeDtypeStruct((2 * BS, down.shape[1]), jnp.float32)
    return pl.pallas_call(
        edge_kernel,
        in_specs=[smem, vmem, vmem, vmem],
        out_specs=[vmem, vmem],
        out_shape=[out, out],
        compiler_params=pltpu.CompilerParams(vmem_limit_bytes=32 * 1024 * 1024),
        cost_estimate=pl.CostEstimate(
            flops=800_000_000, bytes_accessed=8_000_000, transcendentals=0
        ),
        name="edge_tiles",
    )(core, wide, down, up)


def cross_kernel(core, flags, own_ref, got_ref, sum_ref, send_ref):
    total = own_ref[...] + got_ref[...]
    upper, lower = total[:BS], total[BS:]
    first = core[0] == 0
    keep_far = flags[4 * 2 + 1] > 0
    keep_near = flags[5 * 2] > 0
    upper = jnp.where(first | keep_far, upper, 0.0)
    lower = jnp.where(first | keep_near, lower, 0.0)
    sum_ref[:BS] = upper
    sum_ref[BS:] = lower
    send_ref[:HALF] = jnp.where(first, lower, upper).T
    near = jnp.where(keep_near, 1.0, 0.0)
    far = jnp.where(flags[5 * 2 + 1] > 0, 1.0, 0.0)
    row = lax.broadcasted_iota(jnp.int32, (8, BS), 0)
    send_ref[HALF:] = jnp.where(row == 0, near, far)


def cross_sums(core, flags, own, got):
    smem = pl.BlockSpec(memory_space=pltpu.SMEM)
    vmem = pl.BlockSpec(memory_space=pltpu.VMEM)
    return pl.pallas_call(
        cross_kernel,
        in_specs=[smem, smem, vmem, vmem],
        out_specs=[vmem, vmem],
        out_shape=[
            jax.ShapeDtypeStruct((2 * BS, HALF), jnp.float32),
            jax.ShapeDtypeStruct((HALF + 8, BS), jnp.float32),
        ],
        name="cross_sums",
    )(core, flags, own, got)


UPPER_SLOTS = (((0, 1, 2), (3, 4, 6), (5, 7, 8)), ((3, 4, 5), (6, 7, -1), (8, -1, -1)))
LOWER_SLOTS = (((-1, -1), (1, -1), (4, 2)), ((1, 0), (4, 2), (7, 5)))


def band_kernel(core, flags, keep_ref, got_ref, upper_ref, lower_ref):
    for which in range(2):

        @pl.when(core[0] == which)
        def _():
            for row in range(3):
                block = 3 * which + row
                for k, slot in enumerate(UPPER_SLOTS[which][row]):
                    if slot >= 0:
                        tile = keep_ref[slot] + got_ref[slot]
                        if k > 0:
                            tile = jnp.where(flags[block * 2 + k - 1] > 0, tile, 0.0)
                        upper_ref[row * BS:(row + 1) * BS, k * BS:(k + 1) * BS] = tile
                for k, slot in enumerate(LOWER_SLOTS[which][row], 1):
                    if slot >= 0:
                        tile = keep_ref[slot] + got_ref[slot]
                        tile = jnp.where(flags[(block - k) * 2 + k - 1] > 0, tile, 0.0)
                        lower_ref[row * BS:(row + 1) * BS, (k - 1) * BS:k * BS] = tile.T


def local_bands(core, flags, keep, got):
    smem = pl.BlockSpec(memory_space=pltpu.SMEM)
    vmem = pl.BlockSpec(memory_space=pltpu.VMEM)
    return pl.pallas_call(
        band_kernel,
        in_specs=[smem, smem, vmem, vmem],
        out_specs=[vmem, vmem],
        out_shape=[
            jax.ShapeDtypeStruct((3 * BS, 3 * BS), jnp.float32),
            jax.ShapeDtypeStruct((3 * BS, 2 * BS), jnp.float32),
        ],
        compiler_params=pltpu.CompilerParams(vmem_limit_bytes=32 * 1024 * 1024),
        cost_estimate=pl.CostEstimate(
            flops=10_000_000, bytes_accessed=10_000_000, transcendentals=0
        ),
        name="local_bands",
    )(core, flags, keep, got)


def finish_kernel(core, flags, *refs):
    sums, crossed = refs[0:2], refs[2:4]
    upper_ref, lower_ref = refs[6:8]
    first_stage, second_stage, third_stage, sems = refs[8:]
    first = core[0] == 0
    for part in range(2):
        cols = pl.ds(part * HALF, HALF)
        keep_near = jnp.where(first, crossed[part][HALF:HALF + 1, :], 1.0)
        keep_far = jnp.where(first, crossed[part][HALF + 1:HALF + 2, :], 1.0)
        first_stage[:, cols] = jnp.where(keep_near[:, :HALF] > 0, sums[part][:BS], 0.0)
        second_stage[:, cols] = jnp.where(keep_far[:, :HALF] > 0, sums[part][BS:], 0.0)
        third = crossed[part][:HALF, :]
        third_stage[pl.ds(part * HALF, HALF), :] = jnp.where(
            first | (flags[5 * 2 + 1] > 0), third, 0.0
        )

    def copies(targets):
        moves = [
            pltpu.make_async_copy(source, target, sems.at[i])
            for i, (source, target) in enumerate(
                zip((first_stage, second_stage, third_stage), targets)
            )
        ]
        for move in moves:
            move.start()
        for move in moves:
            move.wait()

    @pl.when(first)
    def _():
        copies((
            lower_ref.at[pl.ds(0, BS), pl.ds(0, BS)],
            lower_ref.at[pl.ds(BS, BS), pl.ds(BS, BS)],
            lower_ref.at[pl.ds(0, BS), pl.ds(BS, BS)],
        ))

    @pl.when(core[0] == 1)
    def _():
        copies((
            upper_ref.at[pl.ds(BS, BS), pl.ds(2 * BS, BS)],
            upper_ref.at[pl.ds(2 * BS, BS), pl.ds(BS, BS)],
            upper_ref.at[pl.ds(2 * BS, BS), pl.ds(2 * BS, BS)],
        ))


def finish(core, flags, sums, crossed, upper, lower):
    smem = pl.BlockSpec(memory_space=pltpu.SMEM)
    vmem = pl.BlockSpec(memory_space=pltpu.VMEM)
    any_space = pl.BlockSpec(memory_space=pl.ANY)
    return pl.pallas_call(
        finish_kernel,
        in_specs=[smem, smem, vmem, vmem, vmem, vmem, any_space, any_space],
        out_specs=[any_space, any_space],
        out_shape=[
            jax.ShapeDtypeStruct(upper.shape, upper.dtype),
            jax.ShapeDtypeStruct(lower.shape, lower.dtype),
        ],
        input_output_aliases={6: 0, 7: 1},
        scratch_shapes=[pltpu.VMEM((BS, BS), jnp.float32)] * 3
        + [pltpu.SemaphoreType.DMA((3,))],
        name="finish",
    )(core, flags, *sums, *crossed, upper, lower)


def body(factors, pair_keep):
    chips = lax.axis_size("ao")
    axes = ("ao", "aux")
    upward = [(2 * c + k, 2 * c + 2 + k) for c in range(chips - 1) for k in range(2)]
    downward = [(b, a) for a, b in upward]
    swap = [(2 * c + k, 2 * c + 1 - k) for c in range(chips) for k in range(2)]
    cross = [(2 * c + 1, 2 * c + 2) for c in range(chips - 1)]
    cross = cross + [(b, a) for a, b in cross]

    core = lax.axis_index("aux").astype(jnp.int32)
    core_ref = core.reshape(1)
    flags = pair_keep.reshape(-1)
    g = jnp.swapaxes(factors[0], 0, 1)
    top = (BLOCKS - 1) * BS
    downs, ups = [], []
    for part in range(2):
        at = part * HALF
        downs.append(lax.ppermute(g[:, at:at + HALF], axes, downward))
        ups.append(lax.ppermute(g[:, top + at:top + at + HALF], axes, upward))

    keep, give, wide = local_tiles(core, g)
    got = lax.ppermute(give, axes, swap)
    sums, crossed = [], []
    for part in range(2):
        own, other = edge_tiles(core_ref, wide, downs[part], ups[part])
        arrived = lax.ppermute(other, axes, swap)
        total, send = cross_sums(core_ref, flags, own, arrived)
        sums.append(total)
        crossed.append(lax.ppermute(send, axes, cross))
    upper, lower = local_bands(core_ref, flags, keep, got)
    return tuple(finish(core_ref, flags, sums, crossed, upper, lower))


def solution(mesh):
    in_specs = (P("aux", "ao", None), P("ao", None))
    out_specs = (P(("ao", "aux"), None), P(("ao", "aux"), None))
    return jax.shard_map(body, mesh=mesh, in_specs=in_specs, out_specs=out_specs, check_vma=False)
```

```python
import jax
import jax.numpy as jnp
from jax import lax
from jax.experimental import pallas as pl
from jax.experimental.pallas import tpu as pltpu
from jax.sharding import PartitionSpec as P

BS = 256
BLOCKS = 6
HELD = 3
SLOTS = HELD * HELD
MIB = 1024 * 1024

BORROWED = {(1, 2): 7, (2, 1): 5, (2, 2): 8}
UPPER = (((0, 1, 2), (3, 4, 5), (6, 7, 8)), ((0, 1, 2), (3, 4, -1), (6, -1, -1)))
LOWER = (((-1, -1), (1, -1), (4, 2)), ((5, 7), (1, 8), (4, 2)))

SMEM = pl.BlockSpec(memory_space=pltpu.SMEM)
VMEM = pl.BlockSpec(memory_space=pltpu.VMEM)
ANY = pl.BlockSpec(memory_space=pl.ANY)
OVER_ROWS = (((0,), (0,)), ((), ()))


def cut_kernel(g_ref, one_ref, two_ref, sems):
    core = lax.axis_index("aux")
    last = (BLOCKS - 1) * BS
    moves = [
        pltpu.make_async_copy(
            g_ref.at[:, pl.ds(pl.multiple_of(start, BS), BS)], out, sems.at[i]
        )
        for i, (start, out) in enumerate(((core * last, one_ref), ((1 - core) * last, two_ref)))
    ]
    for move in moves:
        move.start()
    for move in moves:
        move.wait()


def cut(g):
    out = jax.ShapeDtypeStruct((g.shape[0], BS), g.dtype)
    return pl.pallas_call(
        cut_kernel,
        in_specs=[ANY],
        out_specs=[ANY, ANY],
        out_shape=[out, out],
        scratch_shapes=[pltpu.SemaphoreType.DMA((2,))],
        compiler_params=pltpu.CompilerParams(vmem_limit_bytes=52 * MIB),
        cost_estimate=pl.CostEstimate(flops=0, bytes_accessed=3_000_000, transcendentals=0),
        name="cut",
    )(g)


def local_kernel(flags, g_ref, keep_ref, give_ref, mask_ref, held, sems):
    core = lax.axis_index("aux")
    loads = []
    for block in range(BLOCKS):
        cols = pl.ds(block * BS, BS)
        loads.append(pltpu.make_async_copy(g_ref.at[:, cols], held.at[:, cols], sems.at[block]))
    for load in reversed(loads):
        load.start()

    row = lax.broadcasted_iota(jnp.int32, (8, BS), 0)
    near, far, other = flags[0, BLOCKS - 1], flags[1, BLOCKS - 1], flags[1, BLOCKS - 2]
    values = jnp.where(row == 0, near, jnp.where(row == 1, far, other))
    mask_ref[...] = values.astype(jnp.float32)

    def row_of_tiles(m, count):
        left = held[:, pl.ds(pl.multiple_of(m * BS, BS), BS)]
        right = held[:, pl.ds(pl.multiple_of(m * BS, BS), count * BS)]
        tiles = lax.dot_general(left, right, OVER_ROWS, preferred_element_type=jnp.float32)
        owner = m // HELD
        for k in range(count):
            tile = tiles[:, k * BS:(k + 1) * BS]
            if k > 0:
                tile = jnp.where(flags[k - 1, m] > 0, tile, 0.0)
            slot = HELD * (m - HELD * owner) + k

            @pl.when(owner == core)
            def _():
                keep_ref[slot] = tile

            @pl.when(owner != core)
            def _():
                give_ref[slot] = tile

            for (row, offset), borrowed in BORROWED.items():
                if offset == k:

                    @pl.when((m == row) & (core == 1))
                    def _():
                        keep_ref[borrowed] = tile

                    @pl.when((m == row) & (core == 0))
                    def _():
                        give_ref[borrowed] = tile

    for count in (1, 2):
        loads[BLOCKS - count].wait()
        row_of_tiles(jnp.int32(BLOCKS - count), count)

    def step(i, carry):
        m = BLOCKS - 3 - i
        cols = pl.ds(pl.multiple_of(m * BS, BS), BS)
        pltpu.make_async_copy(g_ref.at[:, cols], held.at[:, cols], sems.at[m]).wait()
        row_of_tiles(m, 3)
        return carry

    lax.fori_loop(0, BLOCKS - 2, step, 0)


def local_tiles(flags, g):
    nocc = g.shape[0]
    return pl.pallas_call(
        local_kernel,
        in_specs=[SMEM, ANY],
        out_specs=[VMEM, VMEM, VMEM],
        out_shape=[
            jax.ShapeDtypeStruct((SLOTS, BS, BS), jnp.float32),
            jax.ShapeDtypeStruct((SLOTS, BS, BS), jnp.float32),
            jax.ShapeDtypeStruct((8, BS), jnp.float32),
        ],
        scratch_shapes=[
            pltpu.VMEM((nocc, BLOCKS * BS), jnp.bfloat16),
            pltpu.SemaphoreType.DMA((BLOCKS,)),
        ],
        compiler_params=pltpu.CompilerParams(vmem_limit_bytes=44 * MIB),
        cost_estimate=pl.CostEstimate(
            flops=12_000_000_000, bytes_accessed=20_000_000, transcendentals=0
        ),
        name="local_tiles",
    )(flags, g)


def edge_kernel(g_ref, came_ref, give_ref, turned_ref, one, two, sems):
    core = lax.axis_index("aux")
    far = (BLOCKS - 2) * BS
    loads = []
    for i, (start, held) in enumerate((((1 - core) * far, one), (core * far, two))):
        cols = pl.ds(pl.multiple_of(start, BS), 2 * BS)
        loads.append(pltpu.make_async_copy(g_ref.at[:, cols], held, sems.at[i]))
    for load in loads:
        load.start()
    loads[0].wait()
    give_ref[...] = lax.dot_general(
        one[...], came_ref[...], OVER_ROWS, preferred_element_type=jnp.float32
    )
    loads[1].wait()
    turned_ref[...] = two[...].T


def edge_partial(g, came):
    nocc = g.shape[0]
    return pl.pallas_call(
        edge_kernel,
        in_specs=[ANY, VMEM],
        out_specs=[VMEM, VMEM],
        out_shape=[
            jax.ShapeDtypeStruct((2 * BS, BS), jnp.float32),
            jax.ShapeDtypeStruct((2 * BS, nocc), jnp.bfloat16),
        ],
        scratch_shapes=[pltpu.VMEM((nocc, 2 * BS), jnp.bfloat16)] * 2
        + [pltpu.SemaphoreType.DMA((2,))],
        compiler_params=pltpu.CompilerParams(vmem_limit_bytes=44 * MIB),
        cost_estimate=pl.CostEstimate(
            flops=1_600_000_000, bytes_accessed=8_000_000, transcendentals=0
        ),
        name="edge_partial",
    )(g, came)


def band_kernel(keep_ref, got_ref, upper_ref, lower_ref):
    core = lax.axis_index("aux")
    for which in range(2):

        @pl.when(core == which)
        def _():
            for row in range(HELD):
                for k, slot in enumerate(UPPER[which][row]):
                    if slot >= 0:
                        tile = keep_ref[slot] + got_ref[slot]
                        upper_ref[row * BS:(row + 1) * BS, k * BS:(k + 1) * BS] = tile
                for k, slot in enumerate(LOWER[which][row]):
                    if slot >= 0:
                        tile = keep_ref[slot] + got_ref[slot]
                        lower_ref[row * BS:(row + 1) * BS, k * BS:(k + 1) * BS] = tile.T


def local_bands(keep, got):
    return pl.pallas_call(
        band_kernel,
        in_specs=[VMEM, VMEM],
        out_specs=[VMEM, VMEM],
        out_shape=[
            jax.ShapeDtypeStruct((HELD * BS, 3 * BS), jnp.float32),
            jax.ShapeDtypeStruct((HELD * BS, 2 * BS), jnp.float32),
        ],
        compiler_params=pltpu.CompilerParams(vmem_limit_bytes=24 * MIB),
        cost_estimate=pl.CostEstimate(
            flops=10_000_000, bytes_accessed=12_000_000, transcendentals=0
        ),
        name="local_bands",
    )(keep, got)


def sum_kernel(turned_ref, came_ref, got_ref, mask_ref, sum_ref, send_ref):
    total = jnp.dot(turned_ref[...], came_ref[...], preferred_element_type=jnp.float32)
    first = lax.axis_index("aux") == 0
    near = jnp.where(first, 1.0, mask_ref[0:1, :])
    other_pair = jnp.where(first, 1.0, mask_ref[2:3, :])
    top = jnp.where(other_pair > 0, total[:BS] + got_ref[:BS], 0.0)
    low = jnp.where(near > 0, total[BS:] + got_ref[BS:], 0.0)
    sum_ref[:BS] = top
    sum_ref[BS:] = low
    send_ref[:BS] = jnp.where(first, low, top).T
    send_ref[BS:] = mask_ref[...]


def edge_sum(turned, came, got, mask):
    return pl.pallas_call(
        sum_kernel,
        in_specs=[VMEM] * 4,
        out_specs=[VMEM, VMEM],
        out_shape=[
            jax.ShapeDtypeStruct((2 * BS, BS), jnp.float32),
            jax.ShapeDtypeStruct((BS + 8, BS), jnp.float32),
        ],
        compiler_params=pltpu.CompilerParams(vmem_limit_bytes=16 * MIB),
        cost_estimate=pl.CostEstimate(
            flops=1_600_000_000, bytes_accessed=5_000_000, transcendentals=0
        ),
        name="edge_sum",
    )(turned, came, got, mask)


def finish_kernel(sum_ref, cross_ref, mask_ref, _, __, upper_ref, lower_ref, *scratch):
    stages, sems = scratch[:3], scratch[3]
    core = lax.axis_index("aux")
    first = core == 0
    near = jnp.where(first, cross_ref[BS:BS + 1, :], 1.0)
    far = jnp.where(first, cross_ref[BS + 1:BS + 2, :], 1.0)
    third = jnp.where(first, 1.0, mask_ref[1:2, :])
    stages[0][...] = jnp.where(near > 0, sum_ref[:BS], 0.0)
    stages[1][...] = jnp.where(far > 0, sum_ref[BS:], 0.0)
    stages[2][...] = jnp.where(third > 0, cross_ref[:BS], 0.0)

    def copies(band, places):
        moves = [
            pltpu.make_async_copy(
                stage, band.at[pl.ds(row * BS, BS), pl.ds(col * BS, BS)], sems.at[i]
            )
            for i, (stage, (row, col)) in enumerate(zip(stages, places))
        ]
        for move in moves:
            move.start()
        for move in moves:
            move.wait()

    @pl.when(first)
    def _():
        copies(lower_ref, ((0, 0), (1, 1), (0, 1)))

    @pl.when(core == 1)
    def _():
        copies(upper_ref, ((1, 2), (2, 1), (2, 2)))


def finish(total, crossed, mask, upper, lower):
    return pl.pallas_call(
        finish_kernel,
        in_specs=[VMEM, VMEM, VMEM, ANY, ANY],
        out_specs=[ANY, ANY],
        out_shape=[
            jax.ShapeDtypeStruct(upper.shape, upper.dtype),
            jax.ShapeDtypeStruct(lower.shape, lower.dtype),
        ],
        input_output_aliases={3: 0, 4: 1},
        scratch_shapes=[pltpu.VMEM((BS, BS), jnp.float32)] * 3
        + [pltpu.SemaphoreType.DMA((3,))],
        name="finish",
    )(total, crossed, mask, upper, lower)


def body(factors, pair_keep):
    chips = lax.axis_size("ao")
    axes = ("ao", "aux")
    edges = [(c, c + 1) for c in range(chips - 1)]
    leg_one = [(2 * b, 2 * a) for a, b in edges] + [(2 * a + 1, 2 * b + 1) for a, b in edges]
    leg_two = [(2 * a, 2 * b) for a, b in edges] + [(2 * b + 1, 2 * a + 1) for a, b in edges]
    swap = [(2 * c + k, 2 * c + 1 - k) for c in range(chips) for k in range(2)]
    ahead = [(2 * a + 1, 2 * b) for a, b in edges]
    cross = ahead + [(b, a) for a, b in ahead]

    g = jnp.swapaxes(factors[0], 0, 1)
    flags = jnp.swapaxes(pair_keep, 0, 1)
    one, two = cut(g)
    came_one = lax.ppermute(one, axes, leg_one)
    came_two = lax.ppermute(two, axes, leg_two)
    edge_give, turned = edge_partial(g, came_one)
    edge_got = lax.ppermute(edge_give, axes, swap)
    keep, give, mask = local_tiles(flags, g)
    got = lax.ppermute(give, axes, swap)
    total, send = edge_sum(turned, came_two, edge_got, mask)
    crossed = lax.ppermute(send, axes, cross)
    upper, lower = local_bands(keep, got)
    return tuple(finish(total, crossed, mask, upper, lower))


def solution(mesh):
    in_specs = (P("aux", "ao", None), P("ao", None))
    out_specs = (P(("ao", "aux"), None), P(("ao", "aux"), None))
    return jax.shard_map(body, mesh=mesh, in_specs=in_specs, out_specs=out_specs, check_vma=False)
```

```python
import jax
import jax.numpy as jnp
from jax import lax
from jax.experimental import pallas as pl
from jax.experimental.pallas import tpu as pltpu
from jax.sharding import PartitionSpec as P

BS = 256
BLOCKS = 6
HELD = 3
SLOTS = HELD * HELD
MIB = 1024 * 1024

BORROWED = {(1, 2): 7, (2, 1): 5, (2, 2): 8}
UPPER = (((0, 1, 2), (3, 4, 5), (6, 7, 8)), ((0, 1, 2), (3, 4, -1), (6, -1, -1)))
LOWER = (((-1, -1), (1, -1), (4, 2)), ((5, 7), (1, 8), (4, 2)))

SMEM = pl.BlockSpec(memory_space=pltpu.SMEM)
VMEM = pl.BlockSpec(memory_space=pltpu.VMEM)
ANY = pl.BlockSpec(memory_space=pl.ANY)
OVER_ROWS = (((0,), (0,)), ((), ()))


def cut_kernel(g_ref, out_ref, sem):
    start = pl.multiple_of(lax.axis_index("aux") * ((BLOCKS - 1) * BS), BS)
    move = pltpu.make_async_copy(g_ref.at[:, pl.ds(start, BS)], out_ref, sem)
    move.start()
    move.wait()


def cut(g):
    return pl.pallas_call(
        cut_kernel,
        in_specs=[ANY],
        out_specs=VMEM,
        out_shape=jax.ShapeDtypeStruct((g.shape[0], BS), g.dtype),
        scratch_shapes=[pltpu.SemaphoreType.DMA(())],
        compiler_params=pltpu.CompilerParams(vmem_limit_bytes=52 * MIB),
        cost_estimate=pl.CostEstimate(flops=0, bytes_accessed=3_000_000, transcendentals=0),
        name="cut",
    )(g)


def local_kernel(flags, g_ref, keep_ref, give_ref, mask_ref, two_ref, held, sems):
    core = lax.axis_index("aux")
    loads = []
    for block in range(BLOCKS):
        cols = pl.ds(block * BS, BS)
        loads.append(pltpu.make_async_copy(g_ref.at[:, cols], held.at[:, cols], sems.at[block]))
    for load in reversed(loads):
        load.start()

    start = pl.multiple_of((1 - core) * ((BLOCKS - 1) * BS), BS)
    second = pltpu.make_async_copy(g_ref.at[:, pl.ds(start, BS)], two_ref, sems.at[BLOCKS])
    second.start()

    row = lax.broadcasted_iota(jnp.int32, (8, BS), 0)
    near, far, other = flags[0, BLOCKS - 1], flags[1, BLOCKS - 1], flags[1, BLOCKS - 2]
    values = jnp.where(row == 0, near, jnp.where(row == 1, far, other))
    inside = lax.axis_index("ao") < lax.axis_size("ao") - 1
    mask_ref[...] = jnp.where(inside, values, 0).astype(jnp.float32)

    def row_of_tiles(m, count):
        left = held[:, pl.ds(pl.multiple_of(m * BS, BS), BS)]
        right = held[:, pl.ds(pl.multiple_of(m * BS, BS), count * BS)]
        tiles = lax.dot_general(left, right, OVER_ROWS, preferred_element_type=jnp.float32)
        owner = m // HELD
        for k in range(count):
            tile = tiles[:, k * BS:(k + 1) * BS]
            if k > 0:
                tile = jnp.where(flags[k - 1, m] > 0, tile, 0.0)
            slot = HELD * (m - HELD * owner) + k

            @pl.when(owner == core)
            def _():
                keep_ref[slot] = tile

            @pl.when(owner != core)
            def _():
                give_ref[slot] = tile

            for (row, offset), borrowed in BORROWED.items():
                if offset == k:

                    @pl.when((m == row) & (core == 1))
                    def _():
                        keep_ref[borrowed] = tile

                    @pl.when((m == row) & (core == 0))
                    def _():
                        give_ref[borrowed] = tile

    for count in (1, 2):
        loads[BLOCKS - count].wait()
        row_of_tiles(jnp.int32(BLOCKS - count), count)

    def step(i, carry):
        m = BLOCKS - 3 - i
        cols = pl.ds(pl.multiple_of(m * BS, BS), BS)
        pltpu.make_async_copy(g_ref.at[:, cols], held.at[:, cols], sems.at[m]).wait()
        row_of_tiles(m, 3)
        return carry

    lax.fori_loop(0, BLOCKS - 2, step, 0)
    second.wait()


def local_tiles(flags, g):
    nocc = g.shape[0]
    return pl.pallas_call(
        local_kernel,
        in_specs=[SMEM, ANY],
        out_specs=[VMEM, VMEM, VMEM, VMEM],
        out_shape=[
            jax.ShapeDtypeStruct((SLOTS, BS, BS), jnp.float32),
            jax.ShapeDtypeStruct((SLOTS, BS, BS), jnp.float32),
            jax.ShapeDtypeStruct((8, BS), jnp.float32),
            jax.ShapeDtypeStruct((nocc, BS), jnp.bfloat16),
        ],
        scratch_shapes=[
            pltpu.VMEM((nocc, BLOCKS * BS), jnp.bfloat16),
            pltpu.SemaphoreType.DMA((BLOCKS + 1,)),
        ],
        compiler_params=pltpu.CompilerParams(vmem_limit_bytes=44 * MIB),
        cost_estimate=pl.CostEstimate(
            flops=12_000_000_000, bytes_accessed=20_000_000, transcendentals=0
        ),
        name="local_tiles",
    )(flags, g)


def edge_kernel(g_ref, came_ref, give_ref, turned_ref, one, two, sems):
    core = lax.axis_index("aux")
    far = (BLOCKS - 2) * BS
    loads = []
    for i, (start, held) in enumerate((((1 - core) * far, one), (core * far, two))):
        cols = pl.ds(pl.multiple_of(start, BS), 2 * BS)
        loads.append(pltpu.make_async_copy(g_ref.at[:, cols], held, sems.at[i]))
    for load in loads:
        load.start()
    loads[0].wait()
    give_ref[...] = lax.dot_general(
        one[...], came_ref[...], OVER_ROWS, preferred_element_type=jnp.float32
    )
    loads[1].wait()
    turned_ref[...] = two[...].T


def edge_partial(g, came):
    nocc = g.shape[0]
    return pl.pallas_call(
        edge_kernel,
        in_specs=[ANY, VMEM],
        out_specs=[VMEM, VMEM],
        out_shape=[
            jax.ShapeDtypeStruct((2 * BS, BS), jnp.float32),
            jax.ShapeDtypeStruct((2 * BS, nocc), jnp.bfloat16),
        ],
        scratch_shapes=[pltpu.VMEM((nocc, 2 * BS), jnp.bfloat16)] * 2
        + [pltpu.SemaphoreType.DMA((2,))],
        compiler_params=pltpu.CompilerParams(vmem_limit_bytes=44 * MIB),
        cost_estimate=pl.CostEstimate(
            flops=1_600_000_000, bytes_accessed=8_000_000, transcendentals=0
        ),
        name="edge_partial",
    )(g, came)


def band_kernel(keep_ref, got_ref, upper_ref, lower_ref):
    core = lax.axis_index("aux")
    for which in range(2):

        @pl.when(core == which)
        def _():
            for row in range(HELD):
                for k, slot in enumerate(UPPER[which][row]):
                    if slot >= 0:
                        tile = keep_ref[slot] + got_ref[slot]
                        upper_ref[row * BS:(row + 1) * BS, k * BS:(k + 1) * BS] = tile
                for k, slot in enumerate(LOWER[which][row]):
                    if slot >= 0:
                        tile = keep_ref[slot] + got_ref[slot]
                        lower_ref[row * BS:(row + 1) * BS, k * BS:(k + 1) * BS] = tile.T


def local_bands(keep, got):
    return pl.pallas_call(
        band_kernel,
        in_specs=[VMEM, VMEM],
        out_specs=[VMEM, VMEM],
        out_shape=[
            jax.ShapeDtypeStruct((HELD * BS, 3 * BS), jnp.float32),
            jax.ShapeDtypeStruct((HELD * BS, 2 * BS), jnp.float32),
        ],
        compiler_params=pltpu.CompilerParams(vmem_limit_bytes=24 * MIB),
        cost_estimate=pl.CostEstimate(
            flops=10_000_000, bytes_accessed=12_000_000, transcendentals=0
        ),
        name="local_bands",
    )(keep, got)


def sum_kernel(turned_ref, came_ref, got_ref, mask_ref, sum_ref, send_ref):
    total = jnp.dot(turned_ref[...], came_ref[...], preferred_element_type=jnp.float32)
    first = lax.axis_index("aux") == 0
    near = jnp.where(first, 1.0, mask_ref[0:1, :])
    other_pair = jnp.where(first, 1.0, mask_ref[2:3, :])
    top = jnp.where(other_pair > 0, total[:BS] + got_ref[:BS], 0.0)
    low = jnp.where(near > 0, total[BS:] + got_ref[BS:], 0.0)
    sum_ref[:BS] = top
    sum_ref[BS:] = low
    send_ref[:BS] = jnp.where(first, low, top).T
    send_ref[BS:] = mask_ref[...]


def edge_sum(turned, came, got, mask):
    return pl.pallas_call(
        sum_kernel,
        in_specs=[VMEM] * 4,
        out_specs=[VMEM, VMEM],
        out_shape=[
            jax.ShapeDtypeStruct((2 * BS, BS), jnp.float32),
            jax.ShapeDtypeStruct((BS + 8, BS), jnp.float32),
        ],
        compiler_params=pltpu.CompilerParams(vmem_limit_bytes=16 * MIB),
        cost_estimate=pl.CostEstimate(
            flops=1_600_000_000, bytes_accessed=5_000_000, transcendentals=0
        ),
        name="edge_sum",
    )(turned, came, got, mask)


def finish_kernel(sum_ref, cross_ref, mask_ref, _, __, upper_ref, lower_ref, *scratch):
    stages, sems = scratch[:3], scratch[3]
    core = lax.axis_index("aux")
    first = core == 0
    near = jnp.where(first, cross_ref[BS:BS + 1, :], 1.0)
    far = jnp.where(first, cross_ref[BS + 1:BS + 2, :], 1.0)
    third = jnp.where(first, 1.0, mask_ref[1:2, :])
    stages[0][...] = jnp.where(near > 0, sum_ref[:BS], 0.0)
    stages[1][...] = jnp.where(far > 0, sum_ref[BS:], 0.0)
    stages[2][...] = jnp.where(third > 0, cross_ref[:BS], 0.0)

    def copies(band, places):
        moves = [
            pltpu.make_async_copy(
                stage, band.at[pl.ds(row * BS, BS), pl.ds(col * BS, BS)], sems.at[i]
            )
            for i, (stage, (row, col)) in enumerate(zip(stages, places))
        ]
        for move in moves:
            move.start()
        for move in moves:
            move.wait()

    @pl.when(first)
    def _():
        copies(lower_ref, ((0, 0), (1, 1), (0, 1)))

    @pl.when(core == 1)
    def _():
        copies(upper_ref, ((1, 2), (2, 1), (2, 2)))


def finish(total, crossed, mask, upper, lower):
    return pl.pallas_call(
        finish_kernel,
        in_specs=[VMEM, VMEM, VMEM, ANY, ANY],
        out_specs=[ANY, ANY],
        out_shape=[
            jax.ShapeDtypeStruct(upper.shape, upper.dtype),
            jax.ShapeDtypeStruct(lower.shape, lower.dtype),
        ],
        input_output_aliases={3: 0, 4: 1},
        scratch_shapes=[pltpu.VMEM((BS, BS), jnp.float32)] * 3
        + [pltpu.SemaphoreType.DMA((3,))],
        compiler_params=pltpu.CompilerParams(vmem_limit_bytes=8 * MIB),
        name="finish",
    )(total, crossed, mask, upper, lower)


def body(factors, pair_keep):
    chips = lax.axis_size("ao")
    axes = ("ao", "aux")
    edges = [(c, (c + 1) % chips) for c in range(chips)]
    leg_one = [(2 * b, 2 * a) for a, b in edges] + [(2 * a + 1, 2 * b + 1) for a, b in edges]
    leg_two = [(2 * a, 2 * b) for a, b in edges] + [(2 * b + 1, 2 * a + 1) for a, b in edges]
    swap = [(2 * c + k, 2 * c + 1 - k) for c in range(chips) for k in range(2)]
    cross = [(2 * a + 1, 2 * b) for a, b in edges] + [(2 * b, 2 * a + 1) for a, b in edges]

    g = jnp.swapaxes(factors[0], 0, 1)
    flags = jnp.swapaxes(pair_keep, 0, 1)
    came_one = lax.ppermute(cut(g), axes, leg_one)
    keep, give, mask, two = local_tiles(flags, g)
    came_two = lax.ppermute(two, axes, leg_two)
    edge_give, turned = edge_partial(g, came_one)
    edge_got = lax.ppermute(edge_give, axes, swap)
    got = lax.ppermute(give, axes, swap)
    total, send = edge_sum(turned, came_two, edge_got, mask)
    crossed = lax.ppermute(send, axes, cross)
    upper, lower = local_bands(keep, got)
    return tuple(finish(total, crossed, mask, upper, lower))


def solution(mesh):
    in_specs = (P("aux", "ao", None), P("ao", None))
    out_specs = (P(("ao", "aux"), None), P(("ao", "aux"), None))
    return jax.shard_map(body, mesh=mesh, in_specs=in_specs, out_specs=out_specs, check_vma=False)
```

```python
import functools

import jax
import jax.numpy as jnp
from jax import lax
from jax.experimental import pallas as pl
from jax.experimental.pallas import tpu as pltpu
from jax.sharding import PartitionSpec as P

BS = 256
BLOCKS = 6
HELD = 3
SLOTS = HELD * HELD
MIB = 1024 * 1024

BORROWED = {(1, 2): 7, (2, 1): 5, (2, 2): 8}
UPPER = (((0, 1, 2), (3, 4, 5), (6, 7, 8)), ((0, 1, 2), (3, 4, -1), (6, -1, -1)))
LOWER = (((-1, -1), (1, -1), (4, 2)), ((5, 7), (1, 8), (4, 2)))

SMEM = pl.BlockSpec(memory_space=pltpu.SMEM)
VMEM = pl.BlockSpec(memory_space=pltpu.VMEM)
ANY = pl.BlockSpec(memory_space=pl.ANY)
OVER_ROWS = (((0,), (0,)), ((), ()))


def cut_kernel(g_ref, out_ref, sem, *, swapped):
    core = lax.axis_index("aux")
    count = out_ref.shape[1]
    start = (1 - core if swapped else core) * (BLOCKS * BS - count)
    cols = pl.ds(pl.multiple_of(start, BS), count)
    move = pltpu.make_async_copy(g_ref.at[:, cols], out_ref, sem)
    move.start()
    move.wait()


def cut(name, g, blocks, swapped):
    return pl.pallas_call(
        functools.partial(cut_kernel, swapped=swapped),
        in_specs=[ANY],
        out_specs=VMEM,
        out_shape=jax.ShapeDtypeStruct((g.shape[0], blocks * BS), g.dtype),
        scratch_shapes=[pltpu.SemaphoreType.DMA(())],
        compiler_params=pltpu.CompilerParams(vmem_limit_bytes=52 * MIB),
        cost_estimate=pl.CostEstimate(flops=0, bytes_accessed=1000, transcendentals=0),
        name=name,
    )(g)


def local_kernel(flags, g_ref, keep_ref, give_ref, mask_ref, wide_ref, held, sems):
    core = lax.axis_index("aux")
    loads = []
    for block in range(BLOCKS):
        cols = pl.ds(block * BS, BS)
        loads.append(pltpu.make_async_copy(g_ref.at[:, cols], held.at[:, cols], sems.at[block]))
    for load in reversed(loads):
        load.start()

    start = pl.multiple_of(core * ((BLOCKS - 2) * BS), BS)
    wide = pltpu.make_async_copy(g_ref.at[:, pl.ds(start, 2 * BS)], wide_ref, sems.at[BLOCKS])
    wide.start()

    row = lax.broadcasted_iota(jnp.int32, (8, BS), 0)
    near, far, other = flags[0, BLOCKS - 1], flags[1, BLOCKS - 1], flags[1, BLOCKS - 2]
    values = jnp.where(row == 0, near, jnp.where(row == 1, far, other))
    inside = lax.axis_index("ao") < lax.axis_size("ao") - 1
    mask_ref[...] = jnp.where(inside, values, 0).astype(jnp.float32)

    def row_of_tiles(m, count):
        left = held[:, pl.ds(pl.multiple_of(m * BS, BS), BS)]
        right = held[:, pl.ds(pl.multiple_of(m * BS, BS), count * BS)]
        tiles = lax.dot_general(left, right, OVER_ROWS, preferred_element_type=jnp.float32)
        owner = m // HELD
        for k in range(count):
            tile = tiles[:, k * BS:(k + 1) * BS]
            if k > 0:
                tile = jnp.where(flags[k - 1, m] > 0, tile, 0.0)
            slot = HELD * (m - HELD * owner) + k

            @pl.when(owner == core)
            def _():
                keep_ref[slot] = tile

            @pl.when(owner != core)
            def _():
                give_ref[slot] = tile

            for (row, offset), borrowed in BORROWED.items():
                if offset == k:

                    @pl.when((m == row) & (core == 1))
                    def _():
                        keep_ref[borrowed] = tile

                    @pl.when((m == row) & (core == 0))
                    def _():
                        give_ref[borrowed] = tile

    for count in (1, 2):
        loads[BLOCKS - count].wait()
        row_of_tiles(jnp.int32(BLOCKS - count), count)

    def step(i, carry):
        m = BLOCKS - 3 - i
        cols = pl.ds(pl.multiple_of(m * BS, BS), BS)
        pltpu.make_async_copy(g_ref.at[:, cols], held.at[:, cols], sems.at[m]).wait()
        row_of_tiles(m, 3)
        return carry

    lax.fori_loop(0, BLOCKS - 2, step, 0)
    wide.wait()


def local_tiles(flags, g):
    nocc = g.shape[0]
    return pl.pallas_call(
        local_kernel,
        in_specs=[SMEM, ANY],
        out_specs=[VMEM, VMEM, VMEM, VMEM],
        out_shape=[
            jax.ShapeDtypeStruct((SLOTS, BS, BS), jnp.float32),
            jax.ShapeDtypeStruct((SLOTS, BS, BS), jnp.float32),
            jax.ShapeDtypeStruct((8, BS), jnp.float32),
            jax.ShapeDtypeStruct((nocc, 2 * BS), jnp.bfloat16),
        ],
        scratch_shapes=[
            pltpu.VMEM((nocc, BLOCKS * BS), jnp.bfloat16),
            pltpu.SemaphoreType.DMA((BLOCKS + 1,)),
        ],
        compiler_params=pltpu.CompilerParams(vmem_limit_bytes=44 * MIB),
        cost_estimate=pl.CostEstimate(
            flops=100_000_000_000, bytes_accessed=1000, transcendentals=0
        ),
        name="local_tiles",
    )(flags, g)


def edge_kernel(came_ref, wide_ref, part_ref):
    part_ref[...] = lax.dot_general(
        came_ref[...], wide_ref[...], OVER_ROWS, preferred_element_type=jnp.float32
    )


def edge_partial(came, wide):
    return pl.pallas_call(
        edge_kernel,
        in_specs=[VMEM, VMEM],
        out_specs=VMEM,
        out_shape=jax.ShapeDtypeStruct((BS, 2 * BS), jnp.float32),
        compiler_params=pltpu.CompilerParams(vmem_limit_bytes=16 * MIB),
        cost_estimate=pl.CostEstimate(flops=0, bytes_accessed=1000, transcendentals=0),
        name="edge_partial",
    )(came, wide)


def band_kernel(keep_ref, got_ref, upper_ref, lower_ref):
    core = lax.axis_index("aux")
    for which in range(2):

        @pl.when(core == which)
        def _():
            for row in range(HELD):
                for k, slot in enumerate(UPPER[which][row]):
                    if slot >= 0:
                        tile = keep_ref[slot] + got_ref[slot]
                        upper_ref[row * BS:(row + 1) * BS, k * BS:(k + 1) * BS] = tile
                for k, slot in enumerate(LOWER[which][row]):
                    if slot >= 0:
                        tile = keep_ref[slot] + got_ref[slot]
                        lower_ref[row * BS:(row + 1) * BS, k * BS:(k + 1) * BS] = tile.T


def local_bands(keep, got):
    return pl.pallas_call(
        band_kernel,
        in_specs=[VMEM, VMEM],
        out_specs=[VMEM, VMEM],
        out_shape=[
            jax.ShapeDtypeStruct((HELD * BS, 3 * BS), jnp.float32),
            jax.ShapeDtypeStruct((HELD * BS, 2 * BS), jnp.float32),
        ],
        compiler_params=pltpu.CompilerParams(vmem_limit_bytes=24 * MIB),
        cost_estimate=pl.CostEstimate(
            flops=10_000_000, bytes_accessed=12_000_000, transcendentals=0
        ),
        name="local_bands",
    )(keep, got)


def sum_kernel(came_ref, wide_ref, part_ref, mask_ref, sum_ref, send_ref):
    total = part_ref[...] + lax.dot_general(
        came_ref[...], wide_ref[...], OVER_ROWS, preferred_element_type=jnp.float32
    )
    first = lax.axis_index("aux") == 0
    near = jnp.where(first, 1.0, mask_ref[0:1, :])
    other_pair = jnp.where(first, 1.0, mask_ref[2:3, :])
    left = jnp.where(other_pair > 0, total[:, :BS], 0.0)
    right = jnp.where(near > 0, total[:, BS:], 0.0)
    send_ref[:BS] = jnp.where(first, right, left)
    send_ref[BS:] = jnp.where(first, 0.0, mask_ref[...])
    sum_ref[:BS] = left.T
    sum_ref[BS:] = right.T


def edge_sum(came, wide, part, mask):
    return pl.pallas_call(
        sum_kernel,
        in_specs=[VMEM] * 4,
        out_specs=[VMEM, VMEM],
        out_shape=[
            jax.ShapeDtypeStruct((2 * BS, BS), jnp.float32),
            jax.ShapeDtypeStruct((BS + 8, BS), jnp.float32),
        ],
        compiler_params=pltpu.CompilerParams(vmem_limit_bytes=16 * MIB),
        cost_estimate=pl.CostEstimate(
            flops=50_000_000_000, bytes_accessed=1000, transcendentals=0
        ),
        name="edge_sum",
    )(came, wide, part, mask)


def finish_kernel(sum_ref, cross_ref, mask_ref, _, __, upper_ref, lower_ref, *scratch):
    stages, sems = scratch[:3], scratch[3]
    core = lax.axis_index("aux")
    first = core == 0
    near = jnp.where(first, cross_ref[BS:BS + 1, :], 1.0)
    far = jnp.where(first, cross_ref[BS + 1:BS + 2, :], 1.0)
    third = jnp.where(first, cross_ref[BS + 2:BS + 3, :], mask_ref[1:2, :])
    stages[0][...] = jnp.where(near > 0, sum_ref[:BS], 0.0)
    stages[1][...] = jnp.where(far > 0, sum_ref[BS:], 0.0)
    stages[2][...] = jnp.where(third > 0, cross_ref[:BS], 0.0)

    def copies(band, places):
        moves = [
            pltpu.make_async_copy(
                stage, band.at[pl.ds(row * BS, BS), pl.ds(col * BS, BS)], sems.at[i]
            )
            for i, (stage, (row, col)) in enumerate(zip(stages, places))
        ]
        for move in moves:
            move.start()
        for move in moves:
            move.wait()

    @pl.when(first)
    def _():
        copies(lower_ref, ((0, 0), (1, 1), (0, 1)))

    @pl.when(core == 1)
    def _():
        copies(upper_ref, ((1, 2), (2, 1), (2, 2)))


def finish(total, crossed, mask, upper, lower):
    return pl.pallas_call(
        finish_kernel,
        in_specs=[VMEM, VMEM, VMEM, ANY, ANY],
        out_specs=[ANY, ANY],
        out_shape=[
            jax.ShapeDtypeStruct(upper.shape, upper.dtype),
            jax.ShapeDtypeStruct(lower.shape, lower.dtype),
        ],
        input_output_aliases={3: 0, 4: 1},
        scratch_shapes=[pltpu.VMEM((BS, BS), jnp.float32)] * 3
        + [pltpu.SemaphoreType.DMA((3,))],
        compiler_params=pltpu.CompilerParams(vmem_limit_bytes=8 * MIB),
        name="finish",
    )(total, crossed, mask, upper, lower)


def body(factors, pair_keep):
    chips = lax.axis_size("ao")
    axes = ("ao", "aux")
    edges = [(c, c + 1) for c in range(chips - 1)]
    low, high = 0, 2 * chips - 1
    cross = [(2 * a + 1, 2 * b) for a, b in edges] + [(high, low)]
    cross = cross + [(b, a) for a, b in cross]
    along = [(2 * a, 2 * b) for a, b in edges] + [(2 * b + 1, 2 * a + 1) for a, b in edges]
    along = along + [(low + 1, low), (high - 1, high)]
    swap = [(2 * c + k, 2 * c + 1 - k) for c in range(chips) for k in range(2)]

    g = jnp.swapaxes(factors[0], 0, 1)
    flags = jnp.swapaxes(pair_keep, 0, 1)
    came_one = lax.ppermute(cut("cut_first", g, 1, True), axes, along)
    came_two = lax.ppermute(cut("cut_second", g, 1, False), axes, cross)
    other = lax.ppermute(cut("cut_wide", g, 2, True), axes, swap)
    keep, give, mask, wide = local_tiles(flags, g)
    got = lax.ppermute(give, axes, swap)
    part = edge_partial(came_one, wide)
    total, send = edge_sum(came_two, other, part, mask)
    crossed = lax.ppermute(send, axes, cross)
    upper, lower = local_bands(keep, got)
    return tuple(finish(total, crossed, mask, upper, lower))


def solution(mesh):
    in_specs = (P("aux", "ao", None), P("ao", None))
    out_specs = (P(("ao", "aux"), None), P(("ao", "aux"), None))
    return jax.shard_map(body, mesh=mesh, in_specs=in_specs, out_specs=out_specs, check_vma=False)
```

```python
import functools

import jax
import jax.numpy as jnp
from jax import lax
from jax.experimental import pallas as pl
from jax.experimental.pallas import tpu as pltpu
from jax.sharding import PartitionSpec as P

BS = 256
BLOCKS = 6
HELD = 3
HALF = 128
SLOTS = HELD * HELD
MIB = 1024 * 1024

BORROWED = {(1, 2): 7, (2, 1): 5, (2, 2): 8}
UPPER = (((0, 1, 2), (3, 4, 5), (6, 7, 8)), ((0, 1, 2), (3, 4, -1), (6, -1, -1)))
LOWER = (((-1, -1), (1, -1), (4, 2)), ((5, 7), (1, 8), (4, 2)))

SMEM = pl.BlockSpec(memory_space=pltpu.SMEM)
VMEM = pl.BlockSpec(memory_space=pltpu.VMEM)
ANY = pl.BlockSpec(memory_space=pl.ANY)
OVER_ROWS = (((0,), (0,)), ((), ()))


def cut_kernel(g_ref, *refs, swapped):
    outs, sems = refs[:-1], refs[-1]
    count = outs[0].shape[1]
    core = lax.axis_index("aux")
    start = (1 - core if swapped else core) * (BLOCKS * BS - count * len(outs))
    moves = []
    for i, out_ref in enumerate(outs):
        cols = pl.ds(pl.multiple_of(start + i * count, HALF), count)
        moves.append(pltpu.make_async_copy(g_ref.at[:, cols], out_ref, sems.at[i]))
    for move in moves:
        move.start()
    for move in moves:
        move.wait()


def cut(name, g, columns, pieces, swapped):
    out = jax.ShapeDtypeStruct((g.shape[0], columns // pieces), g.dtype)
    return pl.pallas_call(
        functools.partial(cut_kernel, swapped=swapped),
        in_specs=[ANY],
        out_specs=[VMEM] * pieces,
        out_shape=[out] * pieces,
        scratch_shapes=[pltpu.SemaphoreType.DMA((pieces,))],
        compiler_params=pltpu.CompilerParams(vmem_limit_bytes=52 * MIB),
        cost_estimate=pl.CostEstimate(flops=0, bytes_accessed=1000, transcendentals=0),
        name=name,
    )(g)


def local_kernel(flags, g_ref, keep_ref, give_ref, mask_ref, wide_ref, held, sems):
    core = lax.axis_index("aux")
    loads = []
    for block in range(BLOCKS):
        cols = pl.ds(block * BS, BS)
        loads.append(pltpu.make_async_copy(g_ref.at[:, cols], held.at[:, cols], sems.at[block]))
    for load in reversed(loads):
        load.start()

    start = pl.multiple_of(core * ((BLOCKS - 2) * BS), BS)
    wide = pltpu.make_async_copy(g_ref.at[:, pl.ds(start, 2 * BS)], wide_ref, sems.at[BLOCKS])
    wide.start()

    row = lax.broadcasted_iota(jnp.int32, (8, BS), 0)
    near, far, other = flags[0, BLOCKS - 1], flags[1, BLOCKS - 1], flags[1, BLOCKS - 2]
    values = jnp.where(row == 0, near, jnp.where(row == 1, far, other))
    inside = lax.axis_index("ao") < lax.axis_size("ao") - 1
    mask_ref[...] = jnp.where(inside, values, 0).astype(jnp.float32)

    def row_of_tiles(m, count):
        left = held[:, pl.ds(pl.multiple_of(m * BS, BS), BS)]
        right = held[:, pl.ds(pl.multiple_of(m * BS, BS), count * BS)]
        tiles = lax.dot_general(left, right, OVER_ROWS, preferred_element_type=jnp.float32)
        owner = m // HELD
        for k in range(count):
            tile = tiles[:, k * BS:(k + 1) * BS]
            if k > 0:
                tile = jnp.where(flags[k - 1, m] > 0, tile, 0.0)
            slot = HELD * (m - HELD * owner) + k

            @pl.when(owner == core)
            def _():
                keep_ref[slot] = tile

            @pl.when(owner != core)
            def _():
                give_ref[slot] = tile

            for (row, offset), borrowed in BORROWED.items():
                if offset == k:

                    @pl.when((m == row) & (core == 1))
                    def _():
                        keep_ref[borrowed] = tile

                    @pl.when((m == row) & (core == 0))
                    def _():
                        give_ref[borrowed] = tile

    for count in (1, 2):
        loads[BLOCKS - count].wait()
        row_of_tiles(jnp.int32(BLOCKS - count), count)

    def step(i, carry):
        m = BLOCKS - 3 - i
        cols = pl.ds(pl.multiple_of(m * BS, BS), BS)
        pltpu.make_async_copy(g_ref.at[:, cols], held.at[:, cols], sems.at[m]).wait()
        row_of_tiles(m, 3)
        return carry

    lax.fori_loop(0, BLOCKS - 2, step, 0)
    wide.wait()


def local_tiles(flags, g):
    nocc = g.shape[0]
    return pl.pallas_call(
        local_kernel,
        in_specs=[SMEM, ANY],
        out_specs=[VMEM, VMEM, VMEM, VMEM],
        out_shape=[
            jax.ShapeDtypeStruct((SLOTS, BS, BS), jnp.float32),
            jax.ShapeDtypeStruct((SLOTS, BS, BS), jnp.float32),
            jax.ShapeDtypeStruct((8, BS), jnp.float32),
            jax.ShapeDtypeStruct((nocc, 2 * BS), jnp.bfloat16),
        ],
        scratch_shapes=[
            pltpu.VMEM((nocc, BLOCKS * BS), jnp.bfloat16),
            pltpu.SemaphoreType.DMA((BLOCKS + 1,)),
        ],
        compiler_params=pltpu.CompilerParams(vmem_limit_bytes=44 * MIB),
        cost_estimate=pl.CostEstimate(
            flops=50_000_000_000, bytes_accessed=1000, transcendentals=0
        ),
        name="local_tiles",
    )(flags, g)


def edge_kernel(came_ref, wide_ref, part_ref):
    part_ref[...] = lax.dot_general(
        came_ref[...], wide_ref[...], OVER_ROWS, preferred_element_type=jnp.float32
    )


def edge_partial(came, wide):
    return pl.pallas_call(
        edge_kernel,
        in_specs=[VMEM, VMEM],
        out_specs=VMEM,
        out_shape=jax.ShapeDtypeStruct((BS, 2 * BS), jnp.float32),
        compiler_params=pltpu.CompilerParams(vmem_limit_bytes=16 * MIB),
        cost_estimate=pl.CostEstimate(flops=0, bytes_accessed=1000, transcendentals=0),
        name="edge_partial",
    )(came, wide)


def band_kernel(keep_ref, got_ref, upper_ref, lower_ref):
    core = lax.axis_index("aux")
    for which in range(2):

        @pl.when(core == which)
        def _():
            for row in range(HELD):
                for k, slot in enumerate(UPPER[which][row]):
                    if slot >= 0:
                        tile = keep_ref[slot] + got_ref[slot]
                        upper_ref[row * BS:(row + 1) * BS, k * BS:(k + 1) * BS] = tile
                for k, slot in enumerate(LOWER[which][row]):
                    if slot >= 0:
                        tile = keep_ref[slot] + got_ref[slot]
                        lower_ref[row * BS:(row + 1) * BS, k * BS:(k + 1) * BS] = tile.T


def local_bands(keep, got):
    return pl.pallas_call(
        band_kernel,
        in_specs=[VMEM, VMEM],
        out_specs=[VMEM, VMEM],
        out_shape=[
            jax.ShapeDtypeStruct((HELD * BS, 3 * BS), jnp.float32),
            jax.ShapeDtypeStruct((HELD * BS, 2 * BS), jnp.float32),
        ],
        compiler_params=pltpu.CompilerParams(vmem_limit_bytes=24 * MIB),
        cost_estimate=pl.CostEstimate(
            flops=10_000_000, bytes_accessed=12_000_000, transcendentals=0
        ),
        name="local_bands",
    )(keep, got)


def sum_kernel(came_ref, wide_ref, part_ref, mask_ref, sum_ref, send_ref, *, half):
    total = part_ref[half * HALF:(half + 1) * HALF] + lax.dot_general(
        came_ref[...], wide_ref[...], OVER_ROWS, preferred_element_type=jnp.float32
    )
    first = lax.axis_index("aux") == 0
    near = jnp.where(first, 1.0, mask_ref[0:1, :])
    other_pair = jnp.where(first, 1.0, mask_ref[2:3, :])
    left = jnp.where(other_pair > 0, total[:, :BS], 0.0)
    right = jnp.where(near > 0, total[:, BS:], 0.0)
    send_ref[:HALF] = jnp.where(first, right, left)
    send_ref[HALF:] = jnp.where(first, 0.0, mask_ref[...])
    sum_ref[:BS] = left.T
    sum_ref[BS:] = right.T


def edge_sum(half, came, wide, part, mask):
    return pl.pallas_call(
        functools.partial(sum_kernel, half=half),
        in_specs=[VMEM] * 4,
        out_specs=[VMEM, VMEM],
        out_shape=[
            jax.ShapeDtypeStruct((2 * BS, HALF), jnp.float32),
            jax.ShapeDtypeStruct((HALF + 8, BS), jnp.float32),
        ],
        compiler_params=pltpu.CompilerParams(vmem_limit_bytes=16 * MIB),
        cost_estimate=pl.CostEstimate(
            flops=half * 50_000_000_000, bytes_accessed=1000, transcendentals=0
        ),
        name="edge_sum",
    )(came, wide, part, mask)


def finish_kernel(sum_a, sum_b, cross_a, cross_b, mask_ref, _, __, upper_ref, lower_ref, *scratch):
    stages, sems = scratch[:3], scratch[3]
    core = lax.axis_index("aux")
    first = core == 0
    near = jnp.where(first, cross_a[HALF:HALF + 1, :HALF], 1.0)
    far = jnp.where(first, cross_a[HALF + 1:HALF + 2, :HALF], 1.0)
    third = jnp.where(first, cross_a[HALF + 2:HALF + 3, :], mask_ref[1:2, :])
    for half, (sum_ref, cross_ref) in enumerate(((sum_a, cross_a), (sum_b, cross_b))):
        rows = slice(half * HALF, (half + 1) * HALF)
        stages[0][:, rows] = jnp.where(near > 0, sum_ref[:BS], 0.0)
        stages[1][:, rows] = jnp.where(far > 0, sum_ref[BS:], 0.0)
        stages[2][rows, :] = jnp.where(third > 0, cross_ref[:HALF], 0.0)

    def copies(band, places):
        moves = [
            pltpu.make_async_copy(
                stage, band.at[pl.ds(row * BS, BS), pl.ds(col * BS, BS)], sems.at[i]
            )
            for i, (stage, (row, col)) in enumerate(zip(stages, places))
        ]
        for move in moves:
            move.start()
        for move in moves:
            move.wait()

    @pl.when(first)
    def _():
        copies(lower_ref, ((0, 0), (1, 1), (0, 1)))

    @pl.when(core == 1)
    def _():
        copies(upper_ref, ((1, 2), (2, 1), (2, 2)))


def finish(sums, crossed, mask, upper, lower):
    return pl.pallas_call(
        finish_kernel,
        in_specs=[VMEM] * 5 + [ANY, ANY],
        out_specs=[ANY, ANY],
        out_shape=[
            jax.ShapeDtypeStruct(upper.shape, upper.dtype),
            jax.ShapeDtypeStruct(lower.shape, lower.dtype),
        ],
        input_output_aliases={5: 0, 6: 1},
        scratch_shapes=[pltpu.VMEM((BS, BS), jnp.float32)] * 3
        + [pltpu.SemaphoreType.DMA((3,))],
        compiler_params=pltpu.CompilerParams(vmem_limit_bytes=8 * MIB),
        name="finish",
    )(*sums, *crossed, mask, upper, lower)


def body(factors, pair_keep):
    chips = lax.axis_size("ao")
    axes = ("ao", "aux")
    edges = [(c, c + 1) for c in range(chips - 1)]
    low, high = 0, 2 * chips - 1
    cross = [(2 * a + 1, 2 * b) for a, b in edges] + [(high, low)]
    cross = cross + [(b, a) for a, b in cross]
    along = [(2 * a, 2 * b) for a, b in edges] + [(2 * b + 1, 2 * a + 1) for a, b in edges]
    along = along + [(low + 1, low), (high - 1, high)]
    swap = [(2 * c + k, 2 * c + 1 - k) for c in range(chips) for k in range(2)]

    g = jnp.swapaxes(factors[0], 0, 1)
    flags = jnp.swapaxes(pair_keep, 0, 1)
    came_one = lax.ppermute(cut("cut_first", g, BS, 1, True)[0], axes, along)
    came_two = [lax.ppermute(piece, axes, cross) for piece in cut("cut_second", g, BS, 2, False)]
    other = lax.ppermute(cut("cut_wide", g, 2 * BS, 1, True)[0], axes, swap)
    keep, give, mask, wide = local_tiles(flags, g)
    got = lax.ppermute(give, axes, swap)
    part = edge_partial(came_one, wide)
    sums, crossed = [], []
    for half, came in enumerate(came_two):
        total, send = edge_sum(half, came, other, part, mask)
        sums.append(total)
        crossed.append(lax.ppermute(send, axes, cross))
    upper, lower = local_bands(keep, got)
    return tuple(finish(sums, crossed, mask, upper, lower))


def solution(mesh):
    in_specs = (P("aux", "ao", None), P("ao", None))
    out_specs = (P(("ao", "aux"), None), P(("ao", "aux"), None))
    return jax.shard_map(body, mesh=mesh, in_specs=in_specs, out_specs=out_specs, check_vma=False)
```

```python
import functools

import jax
import jax.numpy as jnp
from jax import lax
from jax.experimental import pallas as pl
from jax.experimental.pallas import tpu as pltpu
from jax.sharding import PartitionSpec as P

BS = 256
BLOCKS = 6
HELD = 3
HALF = 128
HEAD = 512
SLOTS = HELD * HELD
MIB = 1024 * 1024

BORROWED = {(1, 2): 7, (2, 1): 5, (2, 2): 8}
UPPER = (((0, 1, 2), (3, 4, 5), (6, 7, 8)), ((0, 1, 2), (3, 4, -1), (6, -1, -1)))
LOWER = (((-1, -1), (1, -1), (4, 2)), ((5, 7), (1, 8), (4, 2)))

SMEM = pl.BlockSpec(memory_space=pltpu.SMEM)
VMEM = pl.BlockSpec(memory_space=pltpu.VMEM)
ANY = pl.BlockSpec(memory_space=pl.ANY)
OVER_ROWS = (((0,), (0,)), ((), ()))


def cut_kernel(g_ref, *refs, swapped, skip):
    outs, sems = refs[:-1], refs[-1]
    rows, count = outs[0].shape
    core = lax.axis_index("aux")
    start = (1 - core if swapped else core) * (BLOCKS * BS - count * len(outs))
    moves = []
    for i, out_ref in enumerate(outs):
        cols = pl.ds(pl.multiple_of(start + i * count, HALF), count)
        moves.append(pltpu.make_async_copy(g_ref.at[pl.ds(skip, rows), cols], out_ref, sems.at[i]))
    for move in moves:
        move.start()
    for move in moves:
        move.wait()


def cut(name, g, columns, pieces, swapped, rows=None, skip=0):
    out = jax.ShapeDtypeStruct((rows or g.shape[0], columns // pieces), g.dtype)
    return pl.pallas_call(
        functools.partial(cut_kernel, swapped=swapped, skip=skip),
        in_specs=[ANY],
        out_specs=[VMEM] * pieces,
        out_shape=[out] * pieces,
        scratch_shapes=[pltpu.SemaphoreType.DMA((pieces,))],
        compiler_params=pltpu.CompilerParams(vmem_limit_bytes=52 * MIB),
        cost_estimate=pl.CostEstimate(flops=0, bytes_accessed=1000, transcendentals=0),
        name=name,
    )(g)


def local_kernel(flags, g_ref, keep_ref, give_ref, mask_ref, wide_ref, held, sems):
    core = lax.axis_index("aux")
    loads = []
    for block in range(BLOCKS):
        cols = pl.ds(block * BS, BS)
        loads.append(pltpu.make_async_copy(g_ref.at[:, cols], held.at[:, cols], sems.at[block]))
    for load in reversed(loads):
        load.start()

    start = pl.multiple_of(core * ((BLOCKS - 2) * BS), BS)
    wide = pltpu.make_async_copy(g_ref.at[:, pl.ds(start, 2 * BS)], wide_ref, sems.at[BLOCKS])
    wide.start()

    row = lax.broadcasted_iota(jnp.int32, (8, BS), 0)
    near, far, other = flags[0, BLOCKS - 1], flags[1, BLOCKS - 1], flags[1, BLOCKS - 2]
    values = jnp.where(row == 0, near, jnp.where(row == 1, far, other))
    inside = lax.axis_index("ao") < lax.axis_size("ao") - 1
    mask_ref[...] = jnp.where(inside, values, 0).astype(jnp.float32)

    def row_of_tiles(m, count):
        left = held[:, pl.ds(pl.multiple_of(m * BS, BS), BS)]
        right = held[:, pl.ds(pl.multiple_of(m * BS, BS), count * BS)]
        tiles = lax.dot_general(left, right, OVER_ROWS, preferred_element_type=jnp.float32)
        owner = m // HELD
        for k in range(count):
            tile = tiles[:, k * BS:(k + 1) * BS]
            if k > 0:
                tile = jnp.where(flags[k - 1, m] > 0, tile, 0.0)
            slot = HELD * (m - HELD * owner) + k

            @pl.when(owner == core)
            def _():
                keep_ref[slot] = tile

            @pl.when(owner != core)
            def _():
                give_ref[slot] = tile

            for (row, offset), borrowed in BORROWED.items():
                if offset == k:

                    @pl.when((m == row) & (core == 1))
                    def _():
                        keep_ref[borrowed] = tile

                    @pl.when((m == row) & (core == 0))
                    def _():
                        give_ref[borrowed] = tile

    for count in (1, 2):
        loads[BLOCKS - count].wait()
        row_of_tiles(jnp.int32(BLOCKS - count), count)

    def step(i, carry):
        m = BLOCKS - 3 - i
        cols = pl.ds(pl.multiple_of(m * BS, BS), BS)
        pltpu.make_async_copy(g_ref.at[:, cols], held.at[:, cols], sems.at[m]).wait()
        row_of_tiles(m, 3)
        return carry

    lax.fori_loop(0, BLOCKS - 2, step, 0)
    wide.wait()


def local_tiles(flags, g):
    nocc = g.shape[0]
    return pl.pallas_call(
        local_kernel,
        in_specs=[SMEM, ANY],
        out_specs=[VMEM, VMEM, VMEM, VMEM],
        out_shape=[
            jax.ShapeDtypeStruct((SLOTS, BS, BS), jnp.float32),
            jax.ShapeDtypeStruct((SLOTS, BS, BS), jnp.float32),
            jax.ShapeDtypeStruct((8, BS), jnp.float32),
            jax.ShapeDtypeStruct((nocc, 2 * BS), jnp.bfloat16),
        ],
        scratch_shapes=[
            pltpu.VMEM((nocc, BLOCKS * BS), jnp.bfloat16),
            pltpu.SemaphoreType.DMA((BLOCKS + 1,)),
        ],
        compiler_params=pltpu.CompilerParams(vmem_limit_bytes=44 * MIB),
        cost_estimate=pl.CostEstimate(
            flops=50_000_000_000, bytes_accessed=1000, transcendentals=0
        ),
        name="local_tiles",
    )(flags, g)


def over_rows(left, right):
    return lax.dot_general(left, right, OVER_ROWS, preferred_element_type=jnp.float32)


def head_kernel(head_ref, wide_ref, part_ref):
    part_ref[...] = over_rows(head_ref[...], wide_ref[:HEAD])


def rest_kernel(rest_ref, wide_ref, head_ref, part_ref):
    part_ref[...] = head_ref[...] + over_rows(rest_ref[...], wide_ref[HEAD:])


def edge_partial(name, kernel, *args):
    return pl.pallas_call(
        kernel,
        in_specs=[VMEM] * len(args),
        out_specs=VMEM,
        out_shape=jax.ShapeDtypeStruct((BS, 2 * BS), jnp.float32),
        compiler_params=pltpu.CompilerParams(vmem_limit_bytes=16 * MIB),
        cost_estimate=pl.CostEstimate(flops=0, bytes_accessed=1000, transcendentals=0),
        name=name,
    )(*args)


def band_kernel(keep_ref, got_ref, upper_ref, lower_ref):
    core = lax.axis_index("aux")
    for which in range(2):

        @pl.when(core == which)
        def _():
            for row in range(HELD):
                for k, slot in enumerate(UPPER[which][row]):
                    if slot >= 0:
                        tile = keep_ref[slot] + got_ref[slot]
                        upper_ref[row * BS:(row + 1) * BS, k * BS:(k + 1) * BS] = tile
                for k, slot in enumerate(LOWER[which][row]):
                    if slot >= 0:
                        tile = keep_ref[slot] + got_ref[slot]
                        lower_ref[row * BS:(row + 1) * BS, k * BS:(k + 1) * BS] = tile.T


def local_bands(keep, got):
    return pl.pallas_call(
        band_kernel,
        in_specs=[VMEM, VMEM],
        out_specs=[VMEM, VMEM],
        out_shape=[
            jax.ShapeDtypeStruct((HELD * BS, 3 * BS), jnp.float32),
            jax.ShapeDtypeStruct((HELD * BS, 2 * BS), jnp.float32),
        ],
        compiler_params=pltpu.CompilerParams(vmem_limit_bytes=24 * MIB),
        cost_estimate=pl.CostEstimate(
            flops=10_000_000, bytes_accessed=12_000_000, transcendentals=0
        ),
        name="local_bands",
    )(keep, got)


def sum_kernel(came_ref, wide_ref, part_ref, mask_ref, sum_ref, send_ref, *, half):
    total = part_ref[half * HALF:(half + 1) * HALF] + over_rows(came_ref[...], wide_ref[...])
    first = lax.axis_index("aux") == 0
    near = jnp.where(first, 1.0, mask_ref[0:1, :])
    other_pair = jnp.where(first, 1.0, mask_ref[2:3, :])
    left = jnp.where(other_pair > 0, total[:, :BS], 0.0)
    right = jnp.where(near > 0, total[:, BS:], 0.0)
    send_ref[:HALF] = jnp.where(first, right, left)
    send_ref[HALF:] = jnp.where(first, 0.0, mask_ref[...])
    sum_ref[:BS] = left.T
    sum_ref[BS:] = right.T


def edge_sum(half, came, wide, part, mask):
    return pl.pallas_call(
        functools.partial(sum_kernel, half=half),
        in_specs=[VMEM] * 4,
        out_specs=[VMEM, VMEM],
        out_shape=[
            jax.ShapeDtypeStruct((2 * BS, HALF), jnp.float32),
            jax.ShapeDtypeStruct((HALF + 8, BS), jnp.float32),
        ],
        compiler_params=pltpu.CompilerParams(vmem_limit_bytes=16 * MIB),
        cost_estimate=pl.CostEstimate(
            flops=half * 50_000_000_000, bytes_accessed=1000, transcendentals=0
        ),
        name="edge_sum",
    )(came, wide, part, mask)


def finish_kernel(sum_a, sum_b, cross_a, cross_b, mask_ref, _, __, upper_ref, lower_ref, *scratch):
    stages, sems = scratch[:3], scratch[3]
    core = lax.axis_index("aux")
    first = core == 0
    near = jnp.where(first, cross_a[HALF:HALF + 1, :HALF], 1.0)
    far = jnp.where(first, cross_a[HALF + 1:HALF + 2, :HALF], 1.0)
    third = jnp.where(first, cross_a[HALF + 2:HALF + 3, :], mask_ref[1:2, :])
    for half, (sum_ref, cross_ref) in enumerate(((sum_a, cross_a), (sum_b, cross_b))):
        rows = slice(half * HALF, (half + 1) * HALF)
        stages[0][:, rows] = jnp.where(near > 0, sum_ref[:BS], 0.0)
        stages[1][:, rows] = jnp.where(far > 0, sum_ref[BS:], 0.0)
        stages[2][rows, :] = jnp.where(third > 0, cross_ref[:HALF], 0.0)

    def copies(band, places):
        moves = [
            pltpu.make_async_copy(
                stage, band.at[pl.ds(row * BS, BS), pl.ds(col * BS, BS)], sems.at[i]
            )
            for i, (stage, (row, col)) in enumerate(zip(stages, places))
        ]
        for move in moves:
            move.start()
        for move in moves:
            move.wait()

    @pl.when(first)
    def _():
        copies(lower_ref, ((0, 0), (1, 1), (0, 1)))

    @pl.when(core == 1)
    def _():
        copies(upper_ref, ((1, 2), (2, 1), (2, 2)))


def finish(sums, crossed, mask, upper, lower):
    return pl.pallas_call(
        finish_kernel,
        in_specs=[VMEM] * 5 + [ANY, ANY],
        out_specs=[ANY, ANY],
        out_shape=[
            jax.ShapeDtypeStruct(upper.shape, upper.dtype),
            jax.ShapeDtypeStruct(lower.shape, lower.dtype),
        ],
        input_output_aliases={5: 0, 6: 1},
        scratch_shapes=[pltpu.VMEM((BS, BS), jnp.float32)] * 3
        + [pltpu.SemaphoreType.DMA((3,))],
        compiler_params=pltpu.CompilerParams(vmem_limit_bytes=8 * MIB),
        name="finish",
    )(*sums, *crossed, mask, upper, lower)


def body(factors, pair_keep):
    chips = lax.axis_size("ao")
    axes = ("ao", "aux")
    edges = [(c, c + 1) for c in range(chips - 1)]
    low, high = 0, 2 * chips - 1
    cross = [(2 * a + 1, 2 * b) for a, b in edges] + [(high, low)]
    cross = cross + [(b, a) for a, b in cross]
    along = [(2 * a, 2 * b) for a, b in edges] + [(2 * b + 1, 2 * a + 1) for a, b in edges]
    along = along + [(low + 1, low), (high - 1, high)]
    swap = [(2 * c + k, 2 * c + 1 - k) for c in range(chips) for k in range(2)]

    g = jnp.swapaxes(factors[0], 0, 1)
    flags = jnp.swapaxes(pair_keep, 0, 1)
    nocc = g.shape[0]
    head = lax.ppermute(cut("cut_head", g, BS, 1, True, HEAD)[0], axes, along)
    rest = lax.ppermute(cut("cut_rest", g, BS, 1, True, nocc - HEAD, HEAD)[0], axes, along)
    came_two = [lax.ppermute(piece, axes, cross) for piece in cut("cut_second", g, BS, 2, False)]
    other = lax.ppermute(cut("cut_wide", g, 2 * BS, 1, True)[0], axes, swap)
    keep, give, mask, wide = local_tiles(flags, g)
    got = lax.ppermute(give, axes, swap)
    part = edge_partial("edge_head", head_kernel, head, wide)
    part = edge_partial("edge_rest", rest_kernel, rest, wide, part)
    sums, crossed = [], []
    for half, came in enumerate(came_two):
        total, send = edge_sum(half, came, other, part, mask)
        sums.append(total)
        crossed.append(lax.ppermute(send, axes, cross))
    upper, lower = local_bands(keep, got)
    return tuple(finish(sums, crossed, mask, upper, lower))


def solution(mesh):
    in_specs = (P("aux", "ao", None), P("ao", None))
    out_specs = (P(("ao", "aux"), None), P(("ao", "aux"), None))
    return jax.shard_map(body, mesh=mesh, in_specs=in_specs, out_specs=out_specs, check_vma=False)
```

```python
import functools

import jax
import jax.numpy as jnp
from jax import lax
from jax.experimental import pallas as pl
from jax.experimental.pallas import tpu as pltpu
from jax.sharding import PartitionSpec as P

BS = 256
BLOCKS = 6
HELD = 3
HALF = 128
HEAD = 512
SLOTS = HELD * HELD
MIB = 1024 * 1024

BORROWED = {(1, 2): 7, (2, 1): 5, (2, 2): 8}
UPPER = (((0, 1, 2), (3, 4, 5), (6, 7, 8)), ((0, 1, 2), (3, 4, -1), (6, -1, -1)))
LOWER = (((-1, -1), (1, -1), (4, 2)), ((5, 7), (1, 8), (4, 2)))

SMEM = pl.BlockSpec(memory_space=pltpu.SMEM)
VMEM = pl.BlockSpec(memory_space=pltpu.VMEM)
ANY = pl.BlockSpec(memory_space=pl.ANY)
OVER_ROWS = (((0,), (0,)), ((), ()))


def cut_kernel(g_ref, *refs, swapped, skip):
    outs, sems = refs[:-1], refs[-1]
    rows, count = outs[0].shape
    core = lax.axis_index("aux")
    start = (1 - core if swapped else core) * (BLOCKS * BS - count * len(outs))
    moves = []
    for i, out_ref in enumerate(outs):
        cols = pl.ds(pl.multiple_of(start + i * count, HALF), count)
        moves.append(pltpu.make_async_copy(g_ref.at[pl.ds(skip, rows), cols], out_ref, sems.at[i]))
    for move in moves:
        move.start()
    for move in moves:
        move.wait()


def cut(name, g, columns, pieces, swapped, rows=None, skip=0):
    out = jax.ShapeDtypeStruct((rows or g.shape[0], columns // pieces), g.dtype)
    return pl.pallas_call(
        functools.partial(cut_kernel, swapped=swapped, skip=skip),
        in_specs=[ANY],
        out_specs=[VMEM] * pieces,
        out_shape=[out] * pieces,
        scratch_shapes=[pltpu.SemaphoreType.DMA((pieces,))],
        compiler_params=pltpu.CompilerParams(vmem_limit_bytes=52 * MIB),
        cost_estimate=pl.CostEstimate(flops=0, bytes_accessed=1000, transcendentals=0),
        name=name,
    )(g)


def local_kernel(flags, g_ref, keep_ref, give_ref, mask_ref, wide_ref, held, sems):
    core = lax.axis_index("aux")
    loads = []
    for block in range(BLOCKS):
        cols = pl.ds(block * BS, BS)
        loads.append(pltpu.make_async_copy(g_ref.at[:, cols], held.at[:, cols], sems.at[block]))
    for load in reversed(loads):
        load.start()

    start = pl.multiple_of(core * ((BLOCKS - 2) * BS), BS)
    wide = pltpu.make_async_copy(g_ref.at[:, pl.ds(start, 2 * BS)], wide_ref, sems.at[BLOCKS])
    wide.start()

    row = lax.broadcasted_iota(jnp.int32, (8, BS), 0)
    near, far, other = flags[0, BLOCKS - 1], flags[1, BLOCKS - 1], flags[1, BLOCKS - 2]
    values = jnp.where(row == 0, near, jnp.where(row == 1, far, other))
    inside = lax.axis_index("ao") < lax.axis_size("ao") - 1
    mask_ref[...] = jnp.where(inside, values, 0).astype(jnp.float32)

    def row_of_tiles(m, count):
        left = held[:, pl.ds(pl.multiple_of(m * BS, BS), BS)]
        right = held[:, pl.ds(pl.multiple_of(m * BS, BS), count * BS)]
        tiles = lax.dot_general(left, right, OVER_ROWS, preferred_element_type=jnp.float32)
        owner = m // HELD
        for k in range(count):
            tile = tiles[:, k * BS:(k + 1) * BS]
            if k > 0:
                tile = jnp.where(flags[k - 1, m] > 0, tile, 0.0)
            slot = HELD * (m - HELD * owner) + k

            @pl.when(owner == core)
            def _():
                keep_ref[slot] = tile

            @pl.when(owner != core)
            def _():
                give_ref[slot] = tile

            for (row, offset), borrowed in BORROWED.items():
                if offset == k:

                    @pl.when((m == row) & (core == 1))
                    def _():
                        keep_ref[borrowed] = tile

                    @pl.when((m == row) & (core == 0))
                    def _():
                        give_ref[borrowed] = tile

    for count in (1, 2):
        loads[BLOCKS - count].wait()
        row_of_tiles(jnp.int32(BLOCKS - count), count)

    def step(i, carry):
        m = BLOCKS - 3 - i
        cols = pl.ds(pl.multiple_of(m * BS, BS), BS)
        pltpu.make_async_copy(g_ref.at[:, cols], held.at[:, cols], sems.at[m]).wait()
        row_of_tiles(m, 3)
        return carry

    lax.fori_loop(0, BLOCKS - 2, step, 0)
    wide.wait()


def local_tiles(flags, g):
    nocc = g.shape[0]
    return pl.pallas_call(
        local_kernel,
        in_specs=[SMEM, ANY],
        out_specs=[VMEM, VMEM, VMEM, VMEM],
        out_shape=[
            jax.ShapeDtypeStruct((SLOTS, BS, BS), jnp.float32),
            jax.ShapeDtypeStruct((SLOTS, BS, BS), jnp.float32),
            jax.ShapeDtypeStruct((8, BS), jnp.float32),
            jax.ShapeDtypeStruct((nocc, 2 * BS), jnp.bfloat16),
        ],
        scratch_shapes=[
            pltpu.VMEM((nocc, BLOCKS * BS), jnp.bfloat16),
            pltpu.SemaphoreType.DMA((BLOCKS + 1,)),
        ],
        compiler_params=pltpu.CompilerParams(vmem_limit_bytes=44 * MIB),
        cost_estimate=pl.CostEstimate(
            flops=50_000_000_000, bytes_accessed=1000, transcendentals=0
        ),
        name="local_tiles",
    )(flags, g)


def over_rows(left, right):
    return lax.dot_general(left, right, OVER_ROWS, preferred_element_type=jnp.float32)


def head_kernel(head_ref, wide_ref, part_ref):
    part_ref[...] = over_rows(head_ref[...], wide_ref[:HEAD])


def rest_kernel(rest_ref, wide_ref, head_ref, part_ref):
    part_ref[...] = head_ref[...] + over_rows(rest_ref[...], wide_ref[HEAD:])


def edge_partial(name, kernel, *args):
    return pl.pallas_call(
        kernel,
        in_specs=[VMEM] * len(args),
        out_specs=VMEM,
        out_shape=jax.ShapeDtypeStruct((BS, 2 * BS), jnp.float32),
        compiler_params=pltpu.CompilerParams(vmem_limit_bytes=16 * MIB),
        cost_estimate=pl.CostEstimate(flops=0, bytes_accessed=1000, transcendentals=0),
        name=name,
    )(*args)


def band_kernel(keep_ref, got_ref, upper_ref, lower_ref):
    core = lax.axis_index("aux")
    for which in range(2):

        @pl.when(core == which)
        def _():
            for row in range(HELD):
                for k, slot in enumerate(UPPER[which][row]):
                    if slot >= 0:
                        tile = keep_ref[slot] + got_ref[slot]
                        upper_ref[row * BS:(row + 1) * BS, k * BS:(k + 1) * BS] = tile
                for k, slot in enumerate(LOWER[which][row]):
                    if slot >= 0:
                        tile = keep_ref[slot] + got_ref[slot]
                        lower_ref[row * BS:(row + 1) * BS, k * BS:(k + 1) * BS] = tile.T


def local_bands(keep, got):
    return pl.pallas_call(
        band_kernel,
        in_specs=[VMEM, VMEM],
        out_specs=[VMEM, VMEM],
        out_shape=[
            jax.ShapeDtypeStruct((HELD * BS, 3 * BS), jnp.float32),
            jax.ShapeDtypeStruct((HELD * BS, 2 * BS), jnp.float32),
        ],
        compiler_params=pltpu.CompilerParams(vmem_limit_bytes=24 * MIB),
        cost_estimate=pl.CostEstimate(
            flops=10_000_000, bytes_accessed=12_000_000, transcendentals=0
        ),
        name="local_bands",
    )(keep, got)


def sum_kernel(came_ref, wide_ref, part_ref, mask_ref, sum_ref, send_ref, *, half):
    total = part_ref[half * HALF:(half + 1) * HALF] + over_rows(came_ref[...], wide_ref[...])
    first = lax.axis_index("aux") == 0
    near = jnp.where(first, 1.0, mask_ref[0:1, :])
    other_pair = jnp.where(first, 1.0, mask_ref[2:3, :])
    left = jnp.where(other_pair > 0, total[:, :BS], 0.0)
    right = jnp.where(near > 0, total[:, BS:], 0.0)
    send_ref[:HALF] = jnp.where(first, right, left)
    send_ref[HALF:] = jnp.where(first, 0.0, mask_ref[...])
    sum_ref[:BS] = left.T
    sum_ref[BS:] = right.T


def edge_sum(half, came, wide, part, mask):
    return pl.pallas_call(
        functools.partial(sum_kernel, half=half),
        in_specs=[VMEM] * 4,
        out_specs=[VMEM, VMEM],
        out_shape=[
            jax.ShapeDtypeStruct((2 * BS, HALF), jnp.float32),
            jax.ShapeDtypeStruct((HALF + 8, BS), jnp.float32),
        ],
        compiler_params=pltpu.CompilerParams(vmem_limit_bytes=16 * MIB),
        cost_estimate=pl.CostEstimate(
            flops=half * 50_000_000_000, bytes_accessed=1000, transcendentals=0
        ),
        name="edge_sum",
    )(came, wide, part, mask)


def finish_kernel(sum_a, sum_b, cross_a, cross_b, mask_ref, _, __, upper_ref, lower_ref, *scratch):
    stages, sems = scratch[:3], scratch[3]
    core = lax.axis_index("aux")
    first = core == 0
    near = jnp.where(first, cross_a[HALF:HALF + 1, :HALF], 1.0)
    far = jnp.where(first, cross_a[HALF + 1:HALF + 2, :HALF], 1.0)
    third = jnp.where(first, cross_a[HALF + 2:HALF + 3, :], mask_ref[1:2, :])
    def move(i, band, place):
        row, col = place
        target = band.at[pl.ds(row * BS, BS), pl.ds(col * BS, BS)]
        return pltpu.make_async_copy(stages[i], target, sems.at[i])

    places = (((0, 0), (1, 2)), ((1, 1), (2, 1)), ((0, 1), (2, 2)))
    for i, (low, up) in enumerate(places):
        for half, (sum_ref, cross_ref) in enumerate(((sum_a, cross_a), (sum_b, cross_b))):
            part = slice(half * HALF, (half + 1) * HALF)
            if i == 0:
                stages[0][:, part] = jnp.where(near > 0, sum_ref[:BS], 0.0)
            elif i == 1:
                stages[1][:, part] = jnp.where(far > 0, sum_ref[BS:], 0.0)
            else:
                stages[2][part, :] = jnp.where(third > 0, cross_ref[:HALF], 0.0)

        @pl.when(first)
        def _():
            move(i, lower_ref, low).start()

        @pl.when(core == 1)
        def _():
            move(i, upper_ref, up).start()

    @pl.when(first)
    def _():
        for i, (low, up) in enumerate(places):
            move(i, lower_ref, low).wait()

    @pl.when(core == 1)
    def _():
        for i, (low, up) in enumerate(places):
            move(i, upper_ref, up).wait()


def finish(sums, crossed, mask, upper, lower):
    return pl.pallas_call(
        finish_kernel,
        in_specs=[VMEM] * 5 + [ANY, ANY],
        out_specs=[ANY, ANY],
        out_shape=[
            jax.ShapeDtypeStruct(upper.shape, upper.dtype),
            jax.ShapeDtypeStruct(lower.shape, lower.dtype),
        ],
        input_output_aliases={5: 0, 6: 1},
        scratch_shapes=[pltpu.VMEM((BS, BS), jnp.float32)] * 3
        + [pltpu.SemaphoreType.DMA((3,))],
        compiler_params=pltpu.CompilerParams(vmem_limit_bytes=8 * MIB),
        name="finish",
    )(*sums, *crossed, mask, upper, lower)


def body(factors, pair_keep):
    chips = lax.axis_size("ao")
    axes = ("ao", "aux")
    edges = [(c, c + 1) for c in range(chips - 1)]
    low, high = 0, 2 * chips - 1
    cross = [(2 * a + 1, 2 * b) for a, b in edges] + [(high, low)]
    cross = cross + [(b, a) for a, b in cross]
    along = [(2 * a, 2 * b) for a, b in edges] + [(2 * b + 1, 2 * a + 1) for a, b in edges]
    along = along + [(low + 1, low), (high - 1, high)]
    swap = [(2 * c + k, 2 * c + 1 - k) for c in range(chips) for k in range(2)]

    g = jnp.swapaxes(factors[0], 0, 1)
    flags = jnp.swapaxes(pair_keep, 0, 1)
    nocc = g.shape[0]
    head = lax.ppermute(cut("cut_head", g, BS, 1, True, HEAD)[0], axes, along)
    rest = lax.ppermute(cut("cut_rest", g, BS, 1, True, nocc - HEAD, HEAD)[0], axes, along)
    came_two = [lax.ppermute(piece, axes, cross) for piece in cut("cut_second", g, BS, 2, False)]
    other = lax.ppermute(cut("cut_wide", g, 2 * BS, 1, True)[0], axes, swap)
    keep, give, mask, wide = local_tiles(flags, g)
    got = lax.ppermute(give, axes, swap)
    part = edge_partial("edge_head", head_kernel, head, wide)
    part = edge_partial("edge_rest", rest_kernel, rest, wide, part)
    sums, crossed = [], []
    for half, came in enumerate(came_two):
        total, send = edge_sum(half, came, other, part, mask)
        sums.append(total)
        crossed.append(lax.ppermute(send, axes, cross))
    upper, lower = local_bands(keep, got)
    return tuple(finish(sums, crossed, mask, upper, lower))


def solution(mesh):
    in_specs = (P("aux", "ao", None), P("ao", None))
    out_specs = (P(("ao", "aux"), None), P(("ao", "aux"), None))
    return jax.shard_map(body, mesh=mesh, in_specs=in_specs, out_specs=out_specs, check_vma=False)
```
